256 devices in a mesh: expert: 64 (over z, y, core), tensor: 4 (over x).
Axes of the slice: x: 4, y: 4, z: 8, core: 2. Of those that a mesh axis runs over, the one named last changes fastest.
Arguments:
- tokens: bfloat16 [8192, 4096], P('expert'), may hold values from -6 to 6
- routing: int32 [8192, 8], P('expert'), may hold values from 0 to 63, all different within a row; in each aligned block of 128 rows (0 to 127, 128 to 255, ...) at most 20 rows name the same one
- gate_weights: float32 [8192, 8], P('expert'), may hold values from 0.05 to 0.45
- w_gate: bfloat16 [64, 4096, 1536], P('expert', None, 'tensor'), may hold values from -0.09375 to 0.09375
- w_up: bfloat16 [64, 4096, 1536], P('expert', None, 'tensor'), may hold values from -0.09375 to 0.09375
- w_down: bfloat16 [64, 1536, 4096], P('expert', 'tensor'), may hold values from -0.15625 to 0.15625
Outputs:
- mixed: bfloat16 [8192, 4096], P('expert', 'tensor')
The draws below stay inside these ranges and needn't reach their ends.
Inputs may be any that keep to these rules, and one draw needn't show every extreme that they name: `routing`: within the rows of one device (128 tokens) a token never names an expert twice, and no expert is named more than 20 times; in every draw some expert is named exactly 20 times in the rows of some device.
All inputs are finite; a program needn't handle non-finite values.
Results may differ from the reference program's by a relative error of at most 0.015.
Values may be sent and summed in bfloat16 or wider, within the bound.
A program may use at most 128 MiB of HBM per device.

```python
import math
import jax
import jax.numpy as jnp
import numpy as np
from jax import lax

D = 4096
FF = 1536
TOP = 8
TOK_DEV = 128
EXPERTS = 64
TOKENS = 8192
CAP = 20
N_EXPERT = 64
N_TENSOR = 4


def steps_of(rng, extent, pieces, low, high):
    gain, own = 1.0, jax.random.fold_in(rng, 6)
    for dim, blocks in pieces:
        steps = jnp.exp(jax.random.uniform(jax.random.fold_in(own, dim), (blocks,), jnp.float32, low / len(pieces), high / len(pieces)))
        gain = gain * jnp.repeat(steps, extent[dim] // blocks).reshape([-1 if axis == dim else 1 for axis in range(len(extent))])
    return gain


def shared_out(rng, own, number, rows, count, top, bound, skew):
    order = jax.random.permutation(rng, count)
    heavy_load, common = shares(count, rows * top, bound, skew, True), shares(count, rows * top, bound, skew, False)
    places = jnp.arange(count)

    def named(sizes, rotation):
        used = int((sizes > 0).sum())
        fixed = max(1, used // 4)
        passed = fixed + (places - fixed + rotation * (used - fixed)) % max(1, count - fixed)
        return jnp.zeros((count,), jnp.int32).at[order[jnp.where(places < fixed, places, passed)]].set(jnp.asarray(sizes, jnp.int32))

    sizes = jnp.where(number % 4 == 0, named(heavy_load, number // 4), named(common, number - number // 4 - 1))
    mixed = jax.random.permutation(jax.random.fold_in(own, 3), count)
    source_of, sink = mixed[0:count // 2 * 2:2], mixed[1:count // 2 * 2:2]
    room = jnp.minimum(sizes[source_of] - 1, bound - sizes[sink]) // 2
    room = jnp.where((source_of == order[0]) | (sink == order[0]) | (sizes[sink] == 0), 0, jnp.maximum(room, 0))
    passed = jax.random.randint(jax.random.fold_in(own, 4), (count // 2,), 0, 1 << 20) % (room + 1)
    sizes = sizes.at[source_of].add(-passed).at[sink].add(passed)
    labels = jnp.searchsorted(jnp.cumsum(sizes), jnp.arange(rows * top), side="right").astype(jnp.int32)
    grid = labels.reshape(top, rows).T
    grid = grid[jax.random.permutation(jax.random.fold_in(own, 1), rows)]
    rotation = jax.random.randint(jax.random.fold_in(own, 2), (rows, 1), 0, top)
    return jnp.take_along_axis(grid, (jnp.arange(top)[None, :] + rotation) % top, axis=1)


def shares(amount, total, limit, slope, full):
    weights = [(1 << 20) // math.isqrt(rank ** slope) + 1 for rank in range(1, amount + 1)]
    largest = limit if full else min(limit, max(-(-total // amount), total * weights[0] // sum(weights)))
    least = 1 if total - largest >= amount - 1 else 0
    given, spare = [largest] + [least] * (amount - 1), total - largest - least * (amount - 1)
    while spare > 0:
        movable = [i for i in range(1, amount) if given[i] < largest] or [i for i in range(1, amount) if given[i] < limit]
        whole, budget = sum([weights[i] for i in movable]), spare
        for i in movable:
            extra = min(limit - given[i], max(1, budget * weights[i] // whole), spare)
            given[i] = given[i] + extra
            spare = spare - extra
    return np.array(given)


def scatter_about(stream_key, dims, spread, reach, split=(), kind=jnp.bfloat16):
    factor_of = steps_of(stream_key, dims, split, -0.22, 0.18) if split else 1.0
    values = jax.random.normal(stream_key, dims, jnp.float32) * spread * factor_of
    return jnp.minimum(jnp.maximum(values, -reach), reach).astype(kind)


def setup_inputs(seed: int = 0) -> dict:
    seeds = jax.random.split(jax.random.key(seed), 7)
    tokens = scatter_about(seeds[0], (TOKENS, D), 1.0, 6.0, ((0, 64),))
    routing_keys = jax.random.split(jax.random.fold_in(seeds[1], 1), TOKENS // TOK_DEV)
    routing_turns = jax.random.permutation(jax.random.fold_in(seeds[1], 3), TOKENS // TOK_DEV)
    routing = jax.vmap(lambda own, number: shared_out(jax.random.fold_in(seeds[1], 2), own, number, TOK_DEV, EXPERTS, TOP, CAP, 2))(routing_keys, routing_turns).reshape((TOKENS, TOP))
    gate_weights = jnp.clip(0.05 + 0.39999999 * jax.random.uniform(seeds[2], (TOKENS, TOP), jnp.float32) ** steps_of(seeds[2], (TOKENS, TOP), ((0, 64),), -0.2, 0.2), 0.05, 0.45)
    w_gate = scatter_about(seeds[3], (EXPERTS, D, FF), D ** -0.5, 0.09375, ((0, 64), (2, 4)))
    w_up = scatter_about(seeds[4], (EXPERTS, D, FF), D ** -0.5, 0.09375, ((0, 64), (2, 4)))
    w_down = scatter_about(seeds[5], (EXPERTS, FF, D), FF ** -0.5, 0.15625, ((0, 64), (1, 4)))
    return dict(tokens=tokens, routing=routing, gate_weights=gate_weights, w_gate=w_gate, w_up=w_up, w_down=w_down)


def reference(tokens, routing, gate_weights, w_gate, w_up, w_down):
    routes_flat = routing.reshape(-1).astype(jnp.int32)
    gate_flat = gate_weights.reshape(-1)
    counts = jnp.bincount(routes_flat, length=EXPERTS).astype(jnp.int32)
    starts = (jnp.cumsum(counts) - counts).astype(jnp.int32)
    ordering = jnp.argsort(routes_flat, stable=True).astype(jnp.int32)
    max_rows = N_EXPERT * CAP
    padded = jnp.concatenate([ordering, jnp.zeros((max_rows,), jnp.int32)])
    slice_cols = FF // N_TENSOR

    def per_expert(totals, expert_id):
        row_ids = lax.dynamic_slice(padded, (starts[expert_id],), (max_rows,))
        live_rows = jnp.arange(max_rows, dtype=jnp.int32) < counts[expert_id]
        token_ids = (row_ids // TOP).astype(jnp.int32)
        gathered = tokens[token_ids]
        gate_proj = jnp.dot(gathered, w_gate[expert_id], preferred_element_type=jnp.float32)
        up_proj = jnp.dot(gathered, w_up[expert_id], preferred_element_type=jnp.float32)
        hidden = (jax.nn.silu(gate_proj) * up_proj).astype(jnp.bfloat16)
        down_proj = w_down[expert_id]
        summed = jnp.zeros((max_rows, D), jnp.float32)
        for part_index in range(N_TENSOR):
            partial_value = jnp.dot(hidden[:, part_index * slice_cols:(part_index + 1) * slice_cols],
                              down_proj[part_index * slice_cols:(part_index + 1) * slice_cols],
                              preferred_element_type=jnp.float32)
            rounded = lax.optimization_barrier(partial_value.astype(jnp.bfloat16))
            summed = summed + rounded.astype(jnp.float32)
        weights = jnp.where(live_rows, gate_flat[row_ids], jnp.zeros((max_rows,), jnp.float32))
        totals = totals.at[token_ids].add(weights[:, None] * summed)
        return totals, None

    totals, unused = lax.scan(per_expert, jnp.zeros((TOKENS, D), jnp.float32), jnp.arange(EXPERTS, dtype=jnp.int32))
    return totals.astype(jnp.bfloat16)
```

```python
import functools

import jax
import jax.numpy as jnp
from jax import lax
from jax.experimental import pallas as pl
from jax.experimental.pallas import tpu as pltpu
from jax.sharding import PartitionSpec as P

MESH = pl.DeviceIdType.MESH
F32, BF16 = jnp.float32, jnp.bfloat16

NZ = 8
NP = 8
NX = 4
CAP = 20
C = 4
GR = 4 * CAP
ROWS = NP * GR
POS = {0: 0, 1: 1, 2: 2, 7: 3, 3: 4, 4: 5, 5: 6, 6: 7}


def dot(a, b):
    return jnp.dot(a, b, preferred_element_type=F32)


def kernel(tok, rt, gw, wg_h, wu_h, wd_h, out, zbuf, meta, pm, wt, yout, rows, acc, wgu, wd, hid,
           pxin, yret, zrec, fin_a, fin_s, fin_r,
           w_sem, zs, zr, ms, mr, ys, yr, yl, xs, xr, zs2, zr2, ys2, yr2, yl2, xs2, xr2, fs, fr):
    T, D = tok.shape
    Q = D // NX
    w = Q // C
    FF = hid.shape[2]
    ex = lax.axis_index("expert")
    x = lax.axis_index("tensor")
    z, p = ex // NP, ex % NP

    def zdev(step):
        return (lax.rem(z + step + NZ, NZ) * NP + p, x)

    def pdev(d):
        return (z * NP + lax.rem(p + d + NP, NP), x)

    def xdev(step):
        return (ex, lax.rem(x + step + NX, NX))

    def remote(src, dst, s, r, dev):
        return pltpu.make_async_remote_copy(src_ref=src, dst_ref=dst, send_sem=s, recv_sem=r,
                                            device_id=dev, device_id_type=MESH)

    w_copies = [
        pltpu.make_async_copy(wg_h.at[0], wgu.at[:, pl.ds(0, FF)], w_sem.at[0]),
        pltpu.make_async_copy(wu_h.at[0], wgu.at[:, pl.ds(FF, FF)], w_sem.at[1]),
        pltpu.make_async_copy(wd_h.at[0], wd, w_sem.at[2]),
    ]
    for c in w_copies:
        c.start()

    barrier = pltpu.get_barrier_semaphore()
    peers = [zdev(1), zdev(-1), xdev(1), xdev(-1)] + [pdev(d) for d in range(1, NP)]
    for dev in peers:
        pl.semaphore_signal(barrier, inc=1, device_id=dev, device_id_type=MESH)

    lane = lax.broadcasted_iota(jnp.int32, (T, 128), 1)
    sub = lax.broadcasted_iota(jnp.int32, (T, 128), 0)
    a = jnp.zeros((T, 128), F32)
    g = jnp.zeros((T, 128), F32)
    for k in range(rt.shape[1]):
        hit = rt[:, k:k + 1] == lane
        a = a + jnp.where(hit, 1.0, 0.0)
        g = g + jnp.where(hit, gw[:, k:k + 1], 0.0)
    a_t = a.T
    g_t = g.T
    earlier = jnp.where(sub < lane, 1.0, 0.0).astype(BF16)
    rank = jnp.where(a_t > 0.0, dot(a_t.astype(BF16), earlier), -64.0)
    meta[0, 0:64, :] = rank[0:64].astype(BF16)
    meta[0, 64:128, :] = g_t[0:64].astype(BF16)

    acc[...] = jnp.zeros_like(acc)
    pl.semaphore_wait(barrier, len(peers))

    def cols(r, n):
        return pl.multiple_of(lax.rem(x + r, NX) * Q + n * w, w)

    def zcopy(n, way, h):
        src, dst = (h - 1, h) if way == 0 else ((NZ - h + 1) % NZ, NZ - h)
        part = pl.ds(0, 2) if h < 4 else pl.ds(way, 1)
        return remote(zbuf.at[n, part, POS[src]], zbuf.at[n, part, POS[dst]],
                      zs.at[n, way, h - 1], zr.at[n, way, h - 1], zdev(1 if way == 0 else -1))

    def mcopy(way, h):
        src, dst = (h - 1, h) if way == 0 else ((NZ - h + 1) % NZ, NZ - h)
        return remote(meta.at[POS[src]], meta.at[POS[dst]],
                      ms.at[way, h - 1], mr.at[way, h - 1], zdev(1 if way == 0 else -1))

    def zstart(n, h):
        for way in range(2):
            zcopy(n, way, h).start()

        @pl.when(n == 0)
        def _():
            for way in range(2 if h < 4 else 1):
                mcopy(way, h).start()

    def zwait(n, h):
        for way in range(2):
            zcopy(n, way, h).wait_recv()

        @pl.when(n == 0)
        def _():
            for way in range(2 if h < 4 else 1):
                mcopy(way, h).wait_recv()

    def block(ref, n, gi, d, count=1):
        return ref.at[n, pl.ds(0, 2), gi, pl.ds(pl.multiple_of(d * GR, 16), count * GR)]

    def ystart(src, dst, s, r, loc, n, gi, sign):
        def one(d, _):
            remote(block(src, n, gi, d), block(dst, n, gi, d), s.at[n, gi], r.at[n, gi], pdev(sign * d)).start()
            return 0
        lax.fori_loop(1, NP, one, 0)
        pltpu.make_async_copy(block(src, n, gi, 0), block(dst, n, gi, 0), loc.at[n, gi]).start()

    def ywait(src, dst, s, r, loc, n, gi):
        remote(block(src, n, gi, 1, NP - 1), block(dst, n, gi, 1, NP - 1), s.at[n, gi], r.at[n, gi], pdev(1)).wait_recv()
        pltpu.make_async_copy(block(src, n, gi, 0), block(dst, n, gi, 0), loc.at[n, gi]).wait()

    def ysent(src, dst, s, r, n, gi):
        remote(block(src, n, gi, 1, NP - 1), block(dst, n, gi, 1, NP - 1), s.at[n, gi], r.at[n, gi], pdev(1)).wait_send()

    def xcopy(n, gi, way):
        src, dst = (0, 3) if way == 0 else (1, 2)
        return remote(rows.at[n, src, gi], rows.at[n, dst, gi], xs.at[n, gi, way], xr.at[n, gi, way],
                      xdev(1 if way == 0 else -1))

    def build(gi):
        row = lax.broadcasted_iota(jnp.int32, (ROWS, 64), 0)
        d = jnp.zeros((ROWS, 64), jnp.int32)
        for j in range(1, NP):
            d = d + jnp.where(row >= j * GR, 1, 0)
        e_of = z * NP + lax.rem(p + d, NP)
        pick = jnp.where(lax.broadcasted_iota(jnp.int32, (ROWS, 64), 1) == e_of, 1.0, 0.0).astype(BF16)
        row = lax.broadcasted_iota(jnp.int32, (ROWS, 128), 0)
        d = jnp.zeros((ROWS, 128), jnp.int32)
        for j in range(1, NP):
            d = d + jnp.where(row >= j * GR, 1, 0)
        within = (row - d * GR).astype(F32)
        for i in range(4):
            m = meta[4 * gi + i]
            s = dot(pick, m[0:64])
            gx = dot(pick, m[64:128])
            hit = s + float(CAP * i) == within
            pm[gi, :, pl.ds(i * 128, 128)] = jnp.where(hit, 1.0, 0.0).astype(BF16)
            wt[gi, pl.ds(i * 128, 128), :] = jnp.where(hit, gx, 0.0).T.astype(BF16)

    def gather(n, gi):
        for ab in range(2):
            yout[n, ab, gi] = dot(pm[gi], zbuf[n, ab, 4 * gi:4 * gi + 4].reshape(4 * T, w)).astype(BF16)

    def up_to(n, gi, first):
        def one(r, _):
            wk = wgu[pl.ds(cols(r, n), w), :]
            acc[gi] = acc[gi] + dot(rows[n, r, gi], wk)
            return 0
        lax.fori_loop(first, first + 2, one, 0)

    def there(t, _):
        n0, n1, n2, n3 = t, t - 1, t - 2, t - 3
        def on(n):
            return pl.when(jnp.logical_and(n >= 0, n < C))

        @on(n0)
        def _():
            for ab in range(2):
                zbuf[n0, ab, 0] = tok[:, pl.ds(cols(ab, n0), w)]
            zstart(n0, 1)

        @on(n1)
        def _():
            zstart(n1, 3)

        @on(n0)
        def _():
            zwait(n0, 1)
            zstart(n0, 2)

        @on(n1)
        def _():
            zwait(n1, 3)
            zstart(n1, 4)

        @on(n0)
        def _():
            zwait(n0, 2)

            @pl.when(n0 == 0)
            def _():
                build(0)
            gather(n0, 0)
            ystart(yout, rows, ys, yr, yl, n0, 0, 1)

        @on(n1)
        def _():
            zwait(n1, 4)

            @pl.when(n1 == 0)
            def _():
                build(1)
            gather(n1, 1)
            ystart(yout, rows, ys, yr, yl, n1, 1, 1)
            ywait(yout, rows, ys, yr, yl, n1, 0)
            for way in range(2):
                xcopy(n1, 0, way).start()

            @pl.when(n1 == 0)
            def _():
                w_copies[0].wait()
                w_copies[1].wait()
            up_to(n1, 0, 0)

        @on(n2)
        def _():
            ywait(yout, rows, ys, yr, yl, n2, 1)
            for way in range(2):
                xcopy(n2, 1, way).start()
            up_to(n2, 1, 0)
            for way in range(2):
                xcopy(n2, 0, way).wait_recv()
            up_to(n2, 0, 2)

        @on(n3)
        def _():
            for way in range(2):
                xcopy(n3, 1, way).wait_recv()
            up_to(n3, 1, 2)
        return 0

    lax.fori_loop(0, C + 3, there, 0)

    def left(n, _):
        for way in range(2):
            for h in range(1, 5):
                zcopy(n, way, h).wait_send()
        for gi in range(2):
            ysent(yout, rows, ys, yr, n, gi)
            for way in range(2):
                xcopy(n, gi, way).wait_send()
        return 0

    lax.fori_loop(0, C, left, 0)
    for h in range(1, 5):
        for way in range(2 if h < 4 else 1):
            mcopy(way, h).wait_send()

    def activate(i, _):
        for gi in range(2):
            at = pl.ds(pl.multiple_of(i * 64, 64), 64)
            gate = acc[gi, at, 0:FF]
            up = acc[gi, at, FF:2 * FF]
            hid[gi, at, :] = (gate / (1.0 + jnp.exp(-gate)) * up).astype(BF16)
        return 0

    lax.fori_loop(0, ROWS // 64, activate, 0)
    w_copies[2].wait()

    def x2copy(n, gi, way):
        return remote(yout.at[n, way, gi], pxin.at[n, 1 - way, gi], xs2.at[n, gi, way], xr2.at[n, gi, way],
                      xdev(1 if way == 0 else -1))

    def down(n, gi, r):
        return dot(hid[gi], wd[:, pl.ds(cols(r, n), w)])

    def z2copy(n, way, h):
        slot = (3 + h) if way == 0 else (5 - h)
        part = pl.ds(0, 2) if h > 1 else pl.ds(way, 1)
        return remote(zbuf.at[n, part, POS[slot]], zrec.at[n, way, h - 1, part],
                      zs2.at[n, way, h - 1], zr2.at[n, way, h - 1], zdev(1 if way == 0 else -1))

    def z2start(n, h):
        for way in range(2):
            z2copy(n, way, h).start()

    def z2add(n, h):
        for way in range(2):
            z2copy(n, way, h).wait_recv()
            slot = POS[(4 + h) if way == 0 else (4 - h)]
            for ab in range(2) if h > 1 else (way,):
                zbuf[n, ab, slot] = (zbuf[n, ab, slot].astype(F32) + zrec[n, way, h - 1, ab].astype(F32)).astype(BF16)

    def combine(n, gi):
        for ab in range(2):
            s = dot(wt[gi], yret[n, ab, gi])
            zbuf[n, ab, 4 * gi:4 * gi + 4] = s.astype(BF16).reshape(4, T, w)

    def fcopy(n):
        return remote(fin_s.at[n], fin_r.at[n], fs.at[n], fr.at[n], xdev(1))

    def back(t, _):
        n0, n1, n2, n3, n4, n5 = (t - i for i in range(6))
        def on(n):
            return pl.when(jnp.logical_and(n >= 0, n < C))

        @on(n0)
        def _():
            for gi in (1, 0):
                for way in range(2):
                    yout[n0, way, gi] = down(n0, gi, 2 + way).astype(BF16)
                    x2copy(n0, gi, way).start()

        @on(n1)
        def _():
            for gi in (1, 0):
                for ab in range(2):
                    x2copy(n1, gi, 1 - ab).wait_recv()
                    rows[n1, ab, gi] = (down(n1, gi, ab) + pxin[n1, ab, gi].astype(F32)).astype(BF16)
                ystart(rows, yret, ys2, yr2, yl2, n1, gi, -1)

        @on(n2)
        def _():
            ywait(rows, yret, ys2, yr2, yl2, n2, 1)
            combine(n2, 1)
            z2start(n2, 1)

        @on(n3)
        def _():
            z2add(n3, 2)
            z2start(n3, 3)

        @on(n2)
        def _():
            ywait(rows, yret, ys2, yr2, yl2, n2, 0)
            combine(n2, 0)
            z2add(n2, 1)
            z2start(n2, 2)

        @on(n3)
        def _():
            z2add(n3, 3)
            z2start(n3, 4)

        @on(n4)
        def _():
            tot = []
            for way in range(2):
                z2copy(n4, way, 4).wait_recv()
            for ab in range(2):
                tot.append(zbuf[n4, ab, 0].astype(F32) + zrec[n4, 0, 3, ab].astype(F32) + zrec[n4, 1, 3, ab].astype(F32))
            fin_a[n4] = tot[0]
            fin_s[n4] = tot[1].astype(BF16)
            fcopy(n4).start()

        @on(n5)
        def _():
            fcopy(n5).wait_recv()
            out[:, pl.ds(pl.multiple_of(n5 * w, w), w)] = (fin_a[n5] + fin_r[n5].astype(F32)).astype(BF16)
        return 0

    lax.fori_loop(0, C + 5, back, 0)

    def left_back(n, _):
        for way in range(2):
            for h in range(1, 5):
                z2copy(n, way, h).wait_send()
        for gi in range(2):
            ysent(rows, yret, ys2, yr2, n, gi)
            for way in range(2):
                x2copy(n, gi, way).wait_send()
        fcopy(n).wait_send()
        return 0

    lax.fori_loop(0, C, left_back, 0)


def local(tokens, routing, gate_weights, w_gate, w_up, w_down):
    T, D = tokens.shape
    FF = w_gate.shape[2]
    w = D // NX // C
    dma = pltpu.SemaphoreType.DMA
    vm = pl.BlockSpec(memory_space=pltpu.VMEM)
    anyw = pl.BlockSpec(memory_space=pl.ANY)
    return pl.pallas_call(
        kernel,
        out_shape=jax.ShapeDtypeStruct((T, D // NX), BF16),
        in_specs=[vm, vm, vm, anyw, anyw, anyw],
        out_specs=vm,
        scratch_shapes=[
            pltpu.VMEM((C, 2, NZ, T, w), BF16),
            pltpu.VMEM((NZ, 128, 128), BF16),
            pltpu.VMEM((2, ROWS, 4 * T), BF16),
            pltpu.VMEM((2, 4 * T, ROWS), BF16),
            pltpu.VMEM((C, 2, 2, ROWS, w), BF16),
            pltpu.VMEM((C, 4, 2, ROWS, w), BF16),
            pltpu.VMEM((2, ROWS, 2 * FF), F32),
            pltpu.VMEM((D, 2 * FF), BF16),
            pltpu.VMEM((FF, D), BF16),
            pltpu.VMEM((2, ROWS, FF), BF16),
            pltpu.VMEM((C, 2, 2, ROWS, w), BF16),
            pltpu.VMEM((C, 2, 2, ROWS, w), BF16),
            pltpu.VMEM((C, 2, 4, 2, T, w), BF16),
            pltpu.VMEM((C, T, w), F32),
            pltpu.VMEM((C, T, w), BF16),
            pltpu.VMEM((C, T, w), BF16),
            dma((3,)),
            dma((C, 2, 4)), dma((C, 2, 4)),
            dma((2, 4)), dma((2, 4)),
            dma((C, 2)), dma((C, 2)), dma((C, 2)),
            dma((C, 2, 2)), dma((C, 2, 2)),
            dma((C, 2, 4)), dma((C, 2, 4)),
            dma((C, 2)), dma((C, 2)), dma((C, 2)),
            dma((C, 2, 2)), dma((C, 2, 2)),
            dma((C,)), dma((C,)),
        ],
        compiler_params=pltpu.CompilerParams(
            collective_id=0, has_side_effects=True, vmem_limit_bytes=60 * 1024 * 1024
        ),
        cost_estimate=pl.CostEstimate(flops=16_000_000_000, bytes_accessed=11_000_000, transcendentals=500_000),
    )(tokens, routing, gate_weights, w_gate, w_up, w_down)


def solution(mesh):
    return jax.shard_map(
        local,
        mesh=mesh,
        in_specs=(
            P("expert", None),
            P("expert", None),
            P("expert", None),
            P("expert", None, "tensor"),
            P("expert", None, "tensor"),
            P("expert", "tensor", None),
        ),
        out_specs=P("expert", "tensor"),
        check_vma=False,
    )
```

```python
import jax
import jax.numpy as jnp
from jax import lax
from jax.experimental import pallas as pl
from jax.experimental.pallas import tpu as pltpu
from jax.sharding import PartitionSpec as P

MESH = pl.DeviceIdType.MESH
F32, BF16 = jnp.float32, jnp.bfloat16

NZ = 8
NP = 8
NX = 4
HEAD = 16
TAIL = 4
C = 4
U = 5
B = 2 * HEAD
ROWS = NP * B
LY, LX = 2, 4
POS = {0: 0, 1: 1, 7: 2, 2: 3, 6: 4, 3: 5, 5: 6, 4: 7}


def dot(a, b):
    return jnp.dot(a, b, preferred_element_type=F32)


def kernel(rt, gw, tok, wg_h, wu_h, wd_h, out, zbuf, meta, pm, pt, wt, wtt, yout, rows, acc, wgu, wd, hid,
           pxin, yret, zrec, fin_a, fin_s, fin_r,
           w_sem, zs, zr, ms, mr, ys, yr, yl, xs, xr, zs2, zr2, ys2, yr2, yl2, xs2, xr2, fs, fr):
    T, D = tok.shape
    Q = D // NX
    w = Q // C
    FF = hid.shape[2]
    ex = lax.axis_index("expert")
    x = lax.axis_index("tensor")
    z, p = ex // NP, ex % NP

    def zdev(step):
        return (lax.rem(z + step + NZ, NZ) * NP + p, x)

    def pdev(d):
        return (z * NP + lax.rem(p + d + NP, NP), x)

    def xdev(step):
        return (ex, lax.rem(x + step + NX, NX))

    def remote(src, dst, s, r, dev):
        return pltpu.make_async_remote_copy(src_ref=src, dst_ref=dst, send_sem=s, recv_sem=r,
                                            device_id=dev, device_id_type=MESH)

    barrier = pltpu.get_barrier_semaphore()
    peers = [zdev(1), zdev(-1), xdev(1), xdev(-1)] + [pdev(d) for d in range(1, NP)]
    for dev in peers:
        pl.semaphore_signal(barrier, inc=1, device_id=dev, device_id_type=MESH)

    w_copies = [
        pltpu.make_async_copy(wg_h.at[0], wgu.at[:, pl.ds(0, FF)], w_sem.at[0]),
        pltpu.make_async_copy(wu_h.at[0], wgu.at[:, pl.ds(FF, FF)], w_sem.at[1]),
        pltpu.make_async_copy(wd_h.at[0], wd, w_sem.at[2]),
    ]
    for c in w_copies:
        c.start()

    def cols(r, n):
        return pl.multiple_of(lax.rem(x + r, NX) * Q + n * w, w)

    NE = NZ * NP
    expert = lax.broadcasted_iota(jnp.int32, (NE, T), 0)
    a = jnp.zeros((NE, T), F32)
    g = jnp.zeros((NE, T), F32)
    for k in range(rt.shape[0]):
        hit = rt[k:k + 1, :] == expert
        a = a + jnp.where(hit, 1.0, 0.0)
        g = g + jnp.where(hit, gw[k:k + 1, :], 0.0)
    earlier = jnp.where(lax.broadcasted_iota(jnp.int32, (T, T), 0) < lax.broadcasted_iota(jnp.int32, (T, T), 1),
                        1.0, 0.0).astype(BF16)
    rank = jnp.where(a > 0.0, dot(a.astype(BF16), earlier), -64.0)
    meta[0, 0:NE, :] = rank.astype(BF16)
    meta[0, NE:2 * NE, :] = g.astype(BF16)

    def own(n, _):
        for ab in range(2):
            zbuf[n, ab, 0] = tok[:, pl.ds(cols(ab, n), w)]
        return 0

    lax.fori_loop(0, C, own, 0)
    acc[...] = jnp.zeros_like(acc)
    pl.semaphore_wait(barrier, len(peers))

    def zcopy(n, way, h):
        src, dst = (h - 1, h) if way == 0 else ((NZ - h + 1) % NZ, NZ - h)
        part = pl.ds(0, 2) if h < 4 else pl.ds(way, 1)
        return remote(zbuf.at[n, part, POS[src]], zbuf.at[n, part, POS[dst]],
                      zs.at[n, way, h - 1], zr.at[n, way, h - 1], zdev(1 if way == 0 else -1))

    def mcopy(way, h):
        src, dst = (h - 1, h) if way == 0 else ((NZ - h + 1) % NZ, NZ - h)
        return remote(meta.at[POS[src]], meta.at[POS[dst]],
                      ms.at[way, h - 1], mr.at[way, h - 1], zdev(1 if way == 0 else -1))

    def zstart(n, h):
        @pl.when(n == 0)
        def _():
            for way in range(2 if h < 4 else 1):
                mcopy(way, h).start()
        for way in range(2):
            zcopy(n, way, h).start()

    def zwait(n, h):
        @pl.when(n == 0)
        def _():
            for way in range(2 if h < 4 else 1):
                mcopy(way, h).wait_recv()
        for way in range(2):
            zcopy(n, way, h).wait_recv()

    def block(ref, n, u, d, count=1):
        return ref.at[n, pl.ds(0, 2), u, pl.ds(pl.multiple_of(d * B, 16), count * B)]

    def ystart(src, dst, s, r, loc, n, u, sign):
        def one(d, _):
            remote(block(src, n, u, d), block(dst, n, u, d), s.at[n, u], r.at[n, u], pdev(sign * d)).start()
            return 0
        lax.fori_loop(1, NP, one, 0)
        pltpu.make_async_copy(block(src, n, u, 0), block(dst, n, u, 0), loc.at[n, u]).start()

    def ywait(src, dst, s, r, loc, n, u):
        remote(block(src, n, u, 1, NP - 1), block(dst, n, u, 1, NP - 1), s.at[n, u], r.at[n, u], pdev(1)).wait_recv()
        pltpu.make_async_copy(block(src, n, u, 0), block(dst, n, u, 0), loc.at[n, u]).wait()

    def ysent(src, dst, s, r, n, u):
        remote(block(src, n, u, 1, NP - 1), block(dst, n, u, 1, NP - 1), s.at[n, u], r.at[n, u], pdev(1)).wait_send()

    def xcopy(n, u, way):
        src, dst = (0, 3) if way == 0 else (1, 2)
        return remote(rows.at[n, src, u], rows.at[n, dst, u], xs.at[n, u, way], xr.at[n, u, way],
                      xdev(1 if way == 0 else -1))

    def build(pair):
        row = lax.broadcasted_iota(jnp.int32, (ROWS, NE), 0)
        e_of = z * NP + lax.rem(p + lax.shift_right_logical(row, 5), NP)
        pick = jnp.where(lax.broadcasted_iota(jnp.int32, (ROWS, NE), 1) == e_of, 1.0, 0.0).astype(BF16)
        row = lax.broadcasted_iota(jnp.int32, (ROWS, T), 0)
        within = (row & (B - 1)).astype(F32)
        for b in range(2):
            pos = 2 * pair + b
            m = meta[pos]
            s = dot(pick, m[0:NE])
            gx = dot(pick, m[NE:2 * NE])
            head = jnp.logical_and(s + float(HEAD * b) == within, s < float(HEAD))
            tail = jnp.logical_and(s + float(TAIL * pos - HEAD) == within, s >= float(HEAD))
            pm[pair, :, pl.ds(b * T, T)] = jnp.where(head, 1.0, 0.0).astype(BF16)
            pt[:, pl.ds(pos * T, T)] = jnp.where(tail, 1.0, 0.0).astype(BF16)
            wt[pair, pl.ds(b * T, T), :] = jnp.where(head, gx, 0.0).T.astype(BF16)
            wtt[pl.ds(pos * T, T), :] = jnp.where(tail, gx, 0.0).T.astype(BF16)

    def gather(n, u):
        @pl.when(u < U - 1)
        def _():
            for ab in range(2):
                yout[n, ab, u] = dot(pm[u], zbuf[n, ab, pl.ds(2 * u, 2)].reshape(2 * T, w)).astype(BF16)

        @pl.when(u == U - 1)
        def _():
            for ab in range(2):
                yout[n, ab, u] = dot(pt[...], zbuf[n, ab].reshape(NZ * T, w)).astype(BF16)

    def up_to(n, u, first):
        def one(r, _):
            acc[u] = acc[u] + dot(rows[n, r, u], wgu[pl.ds(cols(r, n), w), :])
            return 0
        lax.fori_loop(first, first + 2, one, 0)

    def activate(u):
        def one(i, _):
            at = pl.ds(pl.multiple_of(i * 64, 64), 64)
            gate = acc[u, at, 0:FF]
            hid[u, at, :] = (gate / (1.0 + jnp.exp(-gate)) * acc[u, at, FF:2 * FF]).astype(BF16)
            return 0
        lax.fori_loop(0, ROWS // 64, one, 0)

    def on(i):
        return pl.when(jnp.logical_and(i >= 0, i < U * C))

    for n in range(2):
        zstart(n, 1)

    def there(i, _):
        u, n = lax.div(i, C), lax.rem(i, C)
        j, k = i - LY, i - LX
        ju, jn = lax.div(j, C), lax.rem(j, C)
        ku, kn = lax.div(k, C), lax.rem(k, C)

        @on(i)
        def _():
            for pair in range(4):
                @pl.when(u == pair)
                def _():
                    zwait(n, pair + 1)
                    if pair < 3:
                        zstart(n, pair + 2)
                    if pair == 0:
                        @pl.when(n < C - 2)
                        def _():
                            zstart(n + 2, 1)

                    @pl.when(n == 0)
                    def _():
                        build(pair)
            gather(n, u)
            ystart(yout, rows, ys, yr, yl, n, u, 1)

        @pl.when(i == LY)
        def _():
            w_copies[0].wait()
            w_copies[1].wait()

        @on(j)
        def _():
            ywait(yout, rows, ys, yr, yl, jn, ju)
            for way in range(2):
                xcopy(jn, ju, way).start()
            up_to(jn, ju, 0)

        @on(k)
        def _():
            for way in range(2):
                xcopy(kn, ku, way).wait_recv()
            up_to(kn, ku, 2)

            @pl.when(kn == C - 1)
            def _():
                activate(ku)
        return 0

    lax.fori_loop(0, U * C + LX, there, 0)

    def left(n, _):
        for way in range(2):
            for h in range(1, 5):
                zcopy(n, way, h).wait_send()

        def unit(u, _):
            ysent(yout, rows, ys, yr, n, u)
            for way in range(2):
                xcopy(n, u, way).wait_send()
            return 0
        lax.fori_loop(0, U, unit, 0)
        return 0

    lax.fori_loop(0, C, left, 0)
    for h in range(1, 5):
        for way in range(2 if h < 4 else 1):
            mcopy(way, h).wait_send()
    w_copies[2].wait()

    def x2copy(n, u, way):
        return remote(yout.at[n, way, u], pxin.at[n, 1 - way, u], xs2.at[n, u, way], xr2.at[n, u, way],
                      xdev(1 if way == 0 else -1))

    def down(n, u, r):
        return dot(hid[u], wd[:, pl.ds(cols(r, n), w)])

    def z2copy(n, way, h):
        slot = (3 + h) if way == 0 else (5 - h)
        part = pl.ds(0, 2) if h > 1 else pl.ds(way, 1)
        return remote(zbuf.at[n, part, POS[slot]], zrec.at[n, way, h - 1, part],
                      zs2.at[n, way, h - 1], zr2.at[n, way, h - 1], zdev(1 if way == 0 else -1))

    def z2start(n, h):
        for way in range(2):
            z2copy(n, way, h).start()

    def z2add(n, h):
        for way in range(2):
            z2copy(n, way, h).wait_recv()
            slot = POS[(4 + h) if way == 0 else (4 - h)]
            for ab in range(2) if h > 1 else (way,):
                zbuf[n, ab, slot] = (zbuf[n, ab, slot].astype(F32) + zrec[n, way, h - 1, ab].astype(F32)).astype(BF16)

    def combine(n, u):
        @pl.when(u < U - 1)
        def _():
            at = pl.ds(2 * u, 2)
            for ab in range(2):
                s = dot(wt[u], yret[n, ab, u]).reshape(2, T, w)
                zbuf[n, ab, at] = (zbuf[n, ab, at].astype(F32) + s).astype(BF16)

        @pl.when(u == U - 1)
        def _():
            for ab in range(2):
                zbuf[n, ab] = dot(wtt[...], yret[n, ab, u]).astype(BF16).reshape(NZ, T, w)

    def fcopy(n):
        return remote(fin_s.at[n], fin_r.at[n], fs.at[n], fr.at[n], xdev(1))

    def back(i, _):
        j, k = i - LY, i - LX
        u, n = U - 1 - lax.div(i, C), lax.rem(i, C)
        ju, jn = U - 1 - lax.div(j, C), lax.rem(j, C)
        ku, kn = U - 1 - lax.div(k, C), lax.rem(k, C)

        @on(i)
        def _():
            for way in range(2):
                yout[n, way, u] = down(n, u, 2 + way).astype(BF16)
                x2copy(n, u, way).start()

        @on(j)
        def _():
            for ab in range(2):
                x2copy(jn, ju, 1 - ab).wait_recv()
                rows[jn, ab, ju] = (down(jn, ju, ab) + pxin[jn, ab, ju].astype(F32)).astype(BF16)
            ystart(rows, yret, ys2, yr2, yl2, jn, ju, -1)

        @on(k)
        def _():
            ywait(rows, yret, ys2, yr2, yl2, kn, ku)
            combine(kn, ku)
            for h in range(1, 5):
                @pl.when(ku == 4 - h)
                def _():
                    if h > 1:
                        z2add(kn, h - 1)
                    z2start(kn, h)
        return 0

    lax.fori_loop(0, U * C + LX, back, 0)

    def finish(n, _):
        tot = []
        for way in range(2):
            z2copy(n, way, 4).wait_recv()
        for ab in range(2):
            tot.append(zbuf[n, ab, 0].astype(F32) + zrec[n, 0, 3, ab].astype(F32) + zrec[n, 1, 3, ab].astype(F32))
        fin_s[n] = tot[1].astype(BF16)
        fcopy(n).start()
        fin_a[n] = tot[0]
        return 0

    lax.fori_loop(0, C, finish, 0)

    def write(n, _):
        fcopy(n).wait_recv()
        out[:, pl.ds(pl.multiple_of(n * w, w), w)] = (fin_a[n] + fin_r[n].astype(F32)).astype(BF16)
        return 0

    lax.fori_loop(0, C, write, 0)

    def left_back(n, _):
        for way in range(2):
            for h in range(1, 5):
                z2copy(n, way, h).wait_send()

        def unit(u, _):
            ysent(rows, yret, ys2, yr2, n, u)
            for way in range(2):
                x2copy(n, u, way).wait_send()
            return 0
        lax.fori_loop(0, U, unit, 0)
        fcopy(n).wait_send()
        return 0

    lax.fori_loop(0, C, left_back, 0)


def local(tokens, routing, gate_weights, w_gate, w_up, w_down):
    T, D = tokens.shape
    FF = w_gate.shape[2]
    w = D // NX // C
    dma = pltpu.SemaphoreType.DMA
    vm = pl.BlockSpec(memory_space=pltpu.VMEM)
    anyw = pl.BlockSpec(memory_space=pl.ANY)
    return pl.pallas_call(
        kernel,
        out_shape=jax.ShapeDtypeStruct((T, D // NX), BF16),
        in_specs=[vm, vm, vm, anyw, anyw, anyw],
        out_specs=vm,
        scratch_shapes=[
            pltpu.VMEM((C, 2, NZ, T, w), BF16),
            pltpu.VMEM((NZ, 128, T), BF16),
            pltpu.VMEM((U - 1, ROWS, 2 * T), BF16),
            pltpu.VMEM((ROWS, NZ * T), BF16),
            pltpu.VMEM((U - 1, 2 * T, ROWS), BF16),
            pltpu.VMEM((NZ * T, ROWS), BF16),
            pltpu.VMEM((C, 2, U, ROWS, w), BF16),
            pltpu.VMEM((C, 4, U, ROWS, w), BF16),
            pltpu.VMEM((U, ROWS, 2 * FF), F32),
            pltpu.VMEM((D, 2 * FF), BF16),
            pltpu.VMEM((FF, D), BF16),
            pltpu.VMEM((U, ROWS, FF), BF16),
            pltpu.VMEM((C, 2, U, ROWS, w), BF16),
            pltpu.VMEM((C, 2, U, ROWS, w), BF16),
            pltpu.VMEM((C, 2, 4, 2, T, w), BF16),
            pltpu.VMEM((C, T, w), F32),
            pltpu.VMEM((C, T, w), BF16),
            pltpu.VMEM((C, T, w), BF16),
            dma((3,)),
            dma((C, 2, 4)), dma((C, 2, 4)),
            dma((2, 4)), dma((2, 4)),
            dma((C, U)), dma((C, U)), dma((C, U)),
            dma((C, U, 2)), dma((C, U, 2)),
            dma((C, 2, 4)), dma((C, 2, 4)),
            dma((C, U)), dma((C, U)), dma((C, U)),
            dma((C, U, 2)), dma((C, U, 2)),
            dma((C,)), dma((C,)),
        ],
        compiler_params=pltpu.CompilerParams(
            collective_id=0, has_side_effects=True, vmem_limit_bytes=60 * 1024 * 1024
        ),
        cost_estimate=pl.CostEstimate(flops=16_000_000_000, bytes_accessed=11_000_000, transcendentals=500_000),
    )(routing.T, gate_weights.T, tokens, w_gate, w_up, w_down)


def solution(mesh):
    return jax.shard_map(
        local,
        mesh=mesh,
        in_specs=(
            P("expert", None),
            P("expert", None),
            P("expert", None),
            P("expert", None, "tensor"),
            P("expert", None, "tensor"),
            P("expert", "tensor", None),
        ),
        out_specs=P("expert", "tensor"),
        check_vma=False,
    )
```

```python
import jax
import jax.numpy as jnp
from jax import lax
from jax.experimental import pallas as pl
from jax.experimental.pallas import tpu as pltpu
from jax.sharding import PartitionSpec as P

MESH = pl.DeviceIdType.MESH
F32, BF16 = jnp.float32, jnp.bfloat16

NZ = 8
NP = 8
NX = 4
HEAD = 16
TAIL = 4
C = 4
U = 5
B = 2 * HEAD
ROWS = NP * B
LY, LX = 2, 4
KX, KY = 2, 4
R0 = (U - 1) * C + LX - 1
POS = {0: 0, 1: 1, 7: 2, 2: 3, 6: 4, 3: 5, 5: 6, 4: 7}


def dot(a, b):
    return jnp.dot(a, b, preferred_element_type=F32)


def kernel(rt, gw, tok, wg_h, wu_h, wd_h, out, zbuf, meta, pm, pt, wt, wtt, yout, rows, acc, wgu, wd, hid,
           pxin, yret, zrec, fin_a, fin_s, fin_r,
           w_sem, zs, zr, ms, mr, ys, yr, yl, xs, xr, zs2, zr2, ys2, yr2, yl2, xs2, xr2, fs, fr):
    T, D = tok.shape
    Q = D // NX
    w = Q // C
    FF = hid.shape[2]
    ex = lax.axis_index("expert")
    x = lax.axis_index("tensor")
    z, p = ex // NP, ex % NP

    def zdev(step):
        return (lax.rem(z + step + NZ, NZ) * NP + p, x)

    def pdev(d):
        return (z * NP + lax.rem(p + d + NP, NP), x)

    def xdev(step):
        return (ex, lax.rem(x + step + NX, NX))

    def remote(src, dst, s, r, dev):
        return pltpu.make_async_remote_copy(src_ref=src, dst_ref=dst, send_sem=s, recv_sem=r,
                                            device_id=dev, device_id_type=MESH)

    barrier = pltpu.get_barrier_semaphore()
    peers = [zdev(1), zdev(-1), xdev(1), xdev(-1)] + [pdev(d) for d in range(1, NP)]
    for dev in peers:
        pl.semaphore_signal(barrier, inc=1, device_id=dev, device_id_type=MESH)

    w_copies = [
        pltpu.make_async_copy(wg_h.at[0], wgu.at[:, pl.ds(0, FF)], w_sem.at[0]),
        pltpu.make_async_copy(wu_h.at[0], wgu.at[:, pl.ds(FF, FF)], w_sem.at[1]),
        pltpu.make_async_copy(wd_h.at[0], wd, w_sem.at[2]),
    ]
    for c in w_copies:
        c.start()

    def cols(r, n):
        return pl.multiple_of(lax.rem(x + r, NX) * Q + n * w, w)

    NE = NZ * NP
    expert = lax.broadcasted_iota(jnp.int32, (NE, T), 0)
    a = jnp.zeros((NE, T), F32)
    g = jnp.zeros((NE, T), F32)
    for k in range(rt.shape[0]):
        hit = rt[k:k + 1, :] == expert
        a = a + jnp.where(hit, 1.0, 0.0)
        g = g + jnp.where(hit, gw[k:k + 1, :], 0.0)
    earlier = jnp.where(lax.broadcasted_iota(jnp.int32, (T, T), 0) < lax.broadcasted_iota(jnp.int32, (T, T), 1),
                        1.0, 0.0).astype(BF16)
    rank = jnp.where(a > 0.0, dot(a.astype(BF16), earlier), -64.0)
    meta[0, 0:NE, :] = rank.astype(BF16)
    meta[0, NE:2 * NE, :] = g.astype(BF16)

    def own(n, _):
        for ab in range(2):
            zbuf[n, ab, 0] = tok[:, pl.ds(cols(ab, n), w)]
        return 0

    lax.fori_loop(0, C, own, 0)
    acc[...] = jnp.zeros_like(acc)
    pl.semaphore_wait(barrier, len(peers))

    def zcopy(n, way, h):
        src, dst = (h - 1, h) if way == 0 else ((NZ - h + 1) % NZ, NZ - h)
        part = pl.ds(0, 2) if h < 4 else pl.ds(way, 1)
        return remote(zbuf.at[n, part, POS[src]], zbuf.at[n, part, POS[dst]],
                      zs.at[n, way, h - 1], zr.at[n, way, h - 1], zdev(1 if way == 0 else -1))

    def mcopy(way, h):
        src, dst = (h - 1, h) if way == 0 else ((NZ - h + 1) % NZ, NZ - h)
        return remote(meta.at[POS[src]], meta.at[POS[dst]],
                      ms.at[way, h - 1], mr.at[way, h - 1], zdev(1 if way == 0 else -1))

    def zstart(n, h):
        @pl.when(n == 0)
        def _():
            for way in range(2 if h < 4 else 1):
                mcopy(way, h).start()
        for way in range(2):
            zcopy(n, way, h).start()

    def zwait(n, h):
        @pl.when(n == 0)
        def _():
            for way in range(2 if h < 4 else 1):
                mcopy(way, h).wait_recv()
        for way in range(2):
            zcopy(n, way, h).wait_recv()

    def block(ref, n, u, d, count=1):
        return ref.at[n, pl.ds(0, 2), u, pl.ds(pl.multiple_of(d * B, 16), count * B)]

    def ystart(src, dst, s, r, loc, n, u, sign):
        def one(d, _):
            remote(block(src, n, u, d), block(dst, n, u, d), s.at[n, u], r.at[n, u], pdev(sign * d)).start()
            return 0
        lax.fori_loop(1, NP, one, 0)
        pltpu.make_async_copy(block(src, n, u, 0), block(dst, n, u, 0), loc.at[n, u]).start()

    def ywait(src, dst, s, r, loc, n, u):
        remote(block(src, n, u, 1, NP - 1), block(dst, n, u, 1, NP - 1), s.at[n, u], r.at[n, u], pdev(1)).wait_recv()
        pltpu.make_async_copy(block(src, n, u, 0), block(dst, n, u, 0), loc.at[n, u]).wait()

    def ysent(src, dst, s, r, n, u):
        remote(block(src, n, u, 1, NP - 1), block(dst, n, u, 1, NP - 1), s.at[n, u], r.at[n, u], pdev(1)).wait_send()

    def xcopy(n, u, way):
        src, dst = (0, 3) if way == 0 else (1, 2)
        return remote(rows.at[n, src, u], rows.at[n, dst, u], xs.at[n, u, way], xr.at[n, u, way],
                      xdev(1 if way == 0 else -1))

    def build(pair):
        row = lax.broadcasted_iota(jnp.int32, (ROWS, NE), 0)
        e_of = z * NP + lax.rem(p + lax.shift_right_logical(row, 5), NP)
        pick = jnp.where(lax.broadcasted_iota(jnp.int32, (ROWS, NE), 1) == e_of, 1.0, 0.0).astype(BF16)
        row = lax.broadcasted_iota(jnp.int32, (ROWS, T), 0)
        within = (row & (B - 1)).astype(F32)
        for b in range(2):
            pos = 2 * pair + b
            m = meta[pos]
            s = dot(pick, m[0:NE])
            gx = dot(pick, m[NE:2 * NE])
            head = jnp.logical_and(s + float(HEAD * b) == within, s < float(HEAD))
            tail = jnp.logical_and(s + float(TAIL * pos - HEAD) == within, s >= float(HEAD))
            pm[pair, :, pl.ds(b * T, T)] = jnp.where(head, 1.0, 0.0).astype(BF16)
            pt[:, pl.ds(pos * T, T)] = jnp.where(tail, 1.0, 0.0).astype(BF16)
            wt[pair, pl.ds(b * T, T), :] = jnp.where(head, gx, 0.0).T.astype(BF16)
            wtt[pl.ds(pos * T, T), :] = jnp.where(tail, gx, 0.0).T.astype(BF16)

    def gather(n, u):
        @pl.when(u < U - 1)
        def _():
            for ab in range(2):
                yout[n, ab, u] = dot(pm[u], zbuf[n, ab, pl.ds(2 * u, 2)].reshape(2 * T, w)).astype(BF16)

        @pl.when(u == U - 1)
        def _():
            for ab in range(2):
                yout[n, ab, u] = dot(pt[...], zbuf[n, ab].reshape(NZ * T, w)).astype(BF16)

    def up_to(n, u, first):
        def one(r, _):
            acc[u] = acc[u] + dot(rows[n, r, u], wgu[pl.ds(cols(r, n), w), :])
            return 0
        lax.fori_loop(first, first + 2, one, 0)

    def activate(u):
        def one(i, _):
            at = pl.ds(pl.multiple_of(i * 64, 64), 64)
            gate = acc[u, at, 0:FF]
            hid[u, at, :] = (gate / (1.0 + jnp.exp(-gate)) * acc[u, at, FF:2 * FF]).astype(BF16)
            return 0
        lax.fori_loop(0, ROWS // 64, one, 0)

    def on(i):
        return pl.when(jnp.logical_and(i >= 0, i < U * C))

    def x2copy(n, u, way):
        return remote(yout.at[n, way, u], pxin.at[n, 1 - way, u], xs2.at[n, u, way], xr2.at[n, u, way],
                      xdev(1 if way == 0 else -1))

    def down(n, u, r):
        return dot(hid[u], wd[:, pl.ds(cols(r, n), w)])

    def z2copy(n, way, h):
        slot = (3 + h) if way == 0 else (5 - h)
        part = pl.ds(0, 2) if h > 1 else pl.ds(way, 1)
        return remote(zbuf.at[n, part, POS[slot]], zrec.at[n, way, h - 1, part],
                      zs2.at[n, way, h - 1], zr2.at[n, way, h - 1], zdev(1 if way == 0 else -1))

    def z2start(n, h):
        for way in range(2):
            z2copy(n, way, h).start()

    def z2add(n, h):
        for way in range(2):
            z2copy(n, way, h).wait_recv()
            slot = POS[(4 + h) if way == 0 else (4 - h)]
            for ab in range(2) if h > 1 else (way,):
                zbuf[n, ab, slot] = (zbuf[n, ab, slot].astype(F32) + zrec[n, way, h - 1, ab].astype(F32)).astype(BF16)

    def combine(n, u):
        @pl.when(u < U - 1)
        def _():
            at = pl.ds(2 * u, 2)
            for ab in range(2):
                c = dot(wt[u], yret[n, ab, u]).reshape(2, T, w)
                before = jnp.where(u == 3, 0.0, zbuf[n, ab, at].astype(F32))
                zbuf[n, ab, at] = (before + c).astype(BF16)

        @pl.when(u == U - 1)
        def _():
            for ab in range(2):
                c = dot(wtt[...], yret[n, ab, u]).reshape(NZ, T, w)
                zbuf[n, ab, 0:6] = c[0:6].astype(BF16)
                zbuf[n, ab, 6:8] = (zbuf[n, ab, 6:8].astype(F32) + c[6:8]).astype(BF16)

    def fcopy(n):
        return remote(fin_s.at[n], fin_r.at[n], fs.at[n], fr.at[n], xdev(1))

    for n in range(4):
        zstart(n, 1)

    def step(i, _):
        u, n = lax.div(i, C), lax.rem(i, C)
        j, k = i - LY, i - LX
        ju, jn = lax.div(j, C), lax.rem(j, C)
        ku, kn = lax.div(k, C), lax.rem(k, C)

        @on(i)
        def _():
            for pair in range(4):
                @pl.when(u == pair)
                def _():
                    zwait(n, pair + 1)
                    if pair < 3:
                        zstart(n, pair + 2)

                    @pl.when(n == 0)
                    def _():
                        build(pair)
            gather(n, u)
            ystart(yout, rows, ys, yr, yl, n, u, 1)

        @pl.when(i == LY)
        def _():
            w_copies[0].wait()
            w_copies[1].wait()

        @on(j)
        def _():
            ywait(yout, rows, ys, yr, yl, jn, ju)
            for way in range(2):
                xcopy(jn, ju, way).start()
            up_to(jn, ju, 0)

        @on(k)
        def _():
            for way in range(2):
                xcopy(kn, ku, way).wait_recv()
            up_to(kn, ku, 2)

            @pl.when(kn == C - 1)
            def _():
                activate(ku)

        r = i - R0
        rj, rk = r - KX, r - KY

        def unit(q):
            return jnp.where(q == 0, 3, jnp.where(q == 1, 4, 4 - q))
        ru, rn = unit(lax.div(r, C)), lax.rem(r, C)
        rju, rjn = unit(lax.div(rj, C)), lax.rem(rj, C)
        rku, rkn = unit(lax.div(rk, C)), lax.rem(rk, C)

        @pl.when(r == 0)
        def _():
            w_copies[2].wait()

        @on(r)
        def _():
            ysent(yout, rows, ys, yr, rn, ru)
            for way in range(2):
                yout[rn, way, ru] = down(rn, ru, 2 + way).astype(BF16)
                x2copy(rn, ru, way).start()

        @on(rj)
        def _():
            for ab in range(2):
                xcopy(rjn, rju, ab).wait_send()
                x2copy(rjn, rju, 1 - ab).wait_recv()
                rows[rjn, ab, rju] = (down(rjn, rju, ab) + pxin[rjn, ab, rju].astype(F32)).astype(BF16)
            ystart(rows, yret, ys2, yr2, yl2, rjn, rju, -1)

        @on(rk)
        def _():
            ywait(rows, yret, ys2, yr2, yl2, rkn, rku)

            @pl.when(rku == 3)
            def _():
                for way in range(2):
                    for h in range(1, 5):
                        zcopy(rkn, way, h).wait_send()
            combine(rkn, rku)
            for v, h in ((4, 1), (2, 2), (1, 3), (0, 4)):
                @pl.when(rku == v)
                def _():
                    if h > 1:
                        z2add(rkn, h - 1)
                    z2start(rkn, h)
        return 0

    lax.fori_loop(0, R0 + U * C + KY, step, 0)
    for h in range(1, 5):
        for way in range(2 if h < 4 else 1):
            mcopy(way, h).wait_send()

    def finish(n, _):
        tot = []
        for way in range(2):
            z2copy(n, way, 4).wait_recv()
        for ab in range(2):
            tot.append(zbuf[n, ab, 0].astype(F32) + zrec[n, 0, 3, ab].astype(F32) + zrec[n, 1, 3, ab].astype(F32))
        fin_s[n] = tot[1].astype(BF16)
        fcopy(n).start()
        fin_a[n] = tot[0]
        return 0

    lax.fori_loop(0, C, finish, 0)

    def write(n, _):
        fcopy(n).wait_recv()
        out[:, pl.ds(pl.multiple_of(n * w, w), w)] = (fin_a[n] + fin_r[n].astype(F32)).astype(BF16)
        return 0

    lax.fori_loop(0, C, write, 0)

    def left_back(n, _):
        for way in range(2):
            for h in range(1, 5):
                z2copy(n, way, h).wait_send()

        def unit(u, _):
            ysent(rows, yret, ys2, yr2, n, u)
            for way in range(2):
                x2copy(n, u, way).wait_send()
            return 0
        lax.fori_loop(0, U, unit, 0)
        fcopy(n).wait_send()
        return 0

    lax.fori_loop(0, C, left_back, 0)


def local(tokens, routing, gate_weights, w_gate, w_up, w_down):
    T, D = tokens.shape
    FF = w_gate.shape[2]
    w = D // NX // C
    dma = pltpu.SemaphoreType.DMA
    vm = pl.BlockSpec(memory_space=pltpu.VMEM)
    anyw = pl.BlockSpec(memory_space=pl.ANY)
    return pl.pallas_call(
        kernel,
        out_shape=jax.ShapeDtypeStruct((T, D // NX), BF16),
        in_specs=[vm, vm, vm, anyw, anyw, anyw],
        out_specs=vm,
        scratch_shapes=[
            pltpu.VMEM((C, 2, NZ, T, w), BF16),
            pltpu.VMEM((NZ, 128, T), BF16),
            pltpu.VMEM((U - 1, ROWS, 2 * T), BF16),
            pltpu.VMEM((ROWS, NZ * T), BF16),
            pltpu.VMEM((U - 1, 2 * T, ROWS), BF16),
            pltpu.VMEM((NZ * T, ROWS), BF16),
            pltpu.VMEM((C, 2, U, ROWS, w), BF16),
            pltpu.VMEM((C, 4, U, ROWS, w), BF16),
            pltpu.VMEM((U, ROWS, 2 * FF), F32),
            pltpu.VMEM((D, 2 * FF), BF16),
            pltpu.VMEM((FF, D), BF16),
            pltpu.VMEM((U, ROWS, FF), BF16),
            pltpu.VMEM((C, 2, U, ROWS, w), BF16),
            pltpu.VMEM((C, 2, U, ROWS, w), BF16),
            pltpu.VMEM((C, 2, 4, 2, T, w), BF16),
            pltpu.VMEM((C, T, w), F32),
            pltpu.VMEM((C, T, w), BF16),
            pltpu.VMEM((C, T, w), BF16),
            dma((3,)),
            dma((C, 2, 4)), dma((C, 2, 4)),
            dma((2, 4)), dma((2, 4)),
            dma((C, U)), dma((C, U)), dma((C, U)),
            dma((C, U, 2)), dma((C, U, 2)),
            dma((C, 2, 4)), dma((C, 2, 4)),
            dma((C, U)), dma((C, U)), dma((C, U)),
            dma((C, U, 2)), dma((C, U, 2)),
            dma((C,)), dma((C,)),
        ],
        compiler_params=pltpu.CompilerParams(
            collective_id=0, has_side_effects=True, vmem_limit_bytes=60 * 1024 * 1024
        ),
        cost_estimate=pl.CostEstimate(flops=16_000_000_000, bytes_accessed=11_000_000, transcendentals=500_000),
    )(routing.T, gate_weights.T, tokens, w_gate, w_up, w_down)


def solution(mesh):
    return jax.shard_map(
        local,
        mesh=mesh,
        in_specs=(
            P("expert", None),
            P("expert", None),
            P("expert", None),
            P("expert", None, "tensor"),
            P("expert", None, "tensor"),
            P("expert", "tensor", None),
        ),
        out_specs=P("expert", "tensor"),
        check_vma=False,
    )
```

```python
import jax
import jax.numpy as jnp
from jax import lax
from jax.experimental import pallas as pl
from jax.experimental.pallas import tpu as pltpu
from jax.sharding import PartitionSpec as P

MESH = pl.DeviceIdType.MESH
F32, BF16 = jnp.float32, jnp.bfloat16

NZ = 8
NP = 8
NX = 4
HEAD = 16
TAIL = 4
C = 4
U = 5
B = 2 * HEAD
ROWS = NP * B
LY, LX = 2, 4
KX, KY = 2, 4
S = (U - 1) * C + C // 2
R0 = (U - 2) * C + C // 2 - 1 + LX
POS = {0: 0, 4: 1, 1: 2, 7: 3, 2: 4, 6: 5, 3: 6, 5: 7}


def dot(a, b):
    return jnp.dot(a, b, preferred_element_type=F32)


def kernel(rt, gw, tok, wg_h, wu_h, wd_h, out, zbuf, meta, pm, pt, ph, wt, wtt, yout, rows, acc, wgu, wd, hid,
           pxin, yret, zrec, fin_a, fin_s, fin_r,
           w_sem, zs, zr, ms, mr, ys, yr, yl, xs, xr, zs2, zr2, ys2, yr2, yl2, ys4, yr4, yl4, xs3, xr3, xs2, xr2, fs, fr):
    T, D = tok.shape
    Q = D // NX
    w = Q // C
    FF = hid.shape[2]
    ex = lax.axis_index("expert")
    x = lax.axis_index("tensor")
    z, p = ex // NP, ex % NP

    def zdev(step):
        return (lax.rem(z + step + NZ, NZ) * NP + p, x)

    def pdev(d):
        return (z * NP + lax.rem(p + d + NP, NP), x)

    def xdev(step):
        return (ex, lax.rem(x + step + NX, NX))

    def remote(src, dst, s, r, dev):
        return pltpu.make_async_remote_copy(src_ref=src, dst_ref=dst, send_sem=s, recv_sem=r,
                                            device_id=dev, device_id_type=MESH)

    barrier = pltpu.get_barrier_semaphore()
    peers = [zdev(1), zdev(-1), xdev(1), xdev(-1)] + [pdev(d) for d in range(1, NP)]
    for dev in peers:
        pl.semaphore_signal(barrier, inc=1, device_id=dev, device_id_type=MESH)

    w_copies = [
        pltpu.make_async_copy(wg_h.at[0], wgu.at[:, pl.ds(0, FF)], w_sem.at[0]),
        pltpu.make_async_copy(wu_h.at[0], wgu.at[:, pl.ds(FF, FF)], w_sem.at[1]),
        pltpu.make_async_copy(wd_h.at[0], wd, w_sem.at[2]),
    ]
    for c in w_copies:
        c.start()

    def cols(r, n):
        return pl.multiple_of(lax.rem(x + r, NX) * Q + n * w, w)

    NE = NZ * NP
    expert = lax.broadcasted_iota(jnp.int32, (NE, T), 0)
    a = jnp.zeros((NE, T), F32)
    g = jnp.zeros((NE, T), F32)
    for k in range(rt.shape[0]):
        hit = rt[k:k + 1, :] == expert
        a = a + jnp.where(hit, 1.0, 0.0)
        g = g + jnp.where(hit, gw[k:k + 1, :], 0.0)
    earlier = jnp.where(lax.broadcasted_iota(jnp.int32, (T, T), 0) < lax.broadcasted_iota(jnp.int32, (T, T), 1),
                        1.0, 0.0).astype(BF16)
    rank = jnp.where(a > 0.0, dot(a.astype(BF16), earlier), -64.0)
    meta[0, 0:NE, :] = rank.astype(BF16)
    meta[0, NE:2 * NE, :] = g.astype(BF16)

    def own(n, _):
        for ab in range(2):
            zbuf[n, ab, 0] = tok[:, pl.ds(cols(ab, n), w)]
        return 0

    lax.fori_loop(0, C, own, 0)
    acc[...] = jnp.zeros_like(acc)
    pl.semaphore_wait(barrier, len(peers))

    def zcopy(n, way, h):
        src, dst = (h - 1, h) if way == 0 else ((NZ - h + 1) % NZ, NZ - h)
        part = pl.ds(0, 2) if h < 4 else pl.ds(way, 1)
        return remote(zbuf.at[n, part, POS[src]], zbuf.at[n, part, POS[dst]],
                      zs.at[n, way, h - 1], zr.at[n, way, h - 1], zdev(1 if way == 0 else -1))

    def mcopy(way, h):
        src, dst = (h - 1, h) if way == 0 else ((NZ - h + 1) % NZ, NZ - h)
        return remote(meta.at[POS[src]], meta.at[POS[dst]],
                      ms.at[way, h - 1], mr.at[way, h - 1], zdev(1 if way == 0 else -1))

    def zstart(n, h):
        @pl.when(n == 0)
        def _():
            for way in range(2 if h < 4 else 1):
                mcopy(way, h).start()
        for way in range(2):
            zcopy(n, way, h).start()

    def zwait(n, h):
        @pl.when(n == 0)
        def _():
            for way in range(2 if h < 4 else 1):
                mcopy(way, h).wait_recv()
        for way in range(2):
            zcopy(n, way, h).wait_recv()

    def block(ref, n, u, d, count=1):
        return ref.at[n, pl.ds(0, 2), u, pl.ds(d, count)]

    def half(ref, n, b, d, count=1):
        return ref.at[n, pl.ds(0, 2), 0, pl.ds(d, count), pl.ds(b * HEAD, HEAD)]

    def ystart(src, dst, s, r, loc, n, u, sign, b=None):
        def part(ref, d):
            return block(ref, n, u, d) if b is None else half(ref, n, b, d)

        def one(d, _):
            remote(part(src, d), part(dst, d), s, r, pdev(sign * d)).start()
            return 0
        lax.fori_loop(1, NP, one, 0)
        pltpu.make_async_copy(part(src, 0), part(dst, 0), loc).start()

    def yall(src, dst, s, r, n, u, b=None):
        def part(ref):
            return block(ref, n, u, 1, NP - 1) if b is None else half(ref, n, b, 1, NP - 1)
        return remote(part(src), part(dst), s, r, pdev(1))

    def ywait(src, dst, s, r, loc, n, u, b=None):
        def part(ref):
            return block(ref, n, u, 0) if b is None else half(ref, n, b, 0)
        yall(src, dst, s, r, n, u, b).wait_recv()
        pltpu.make_async_copy(part(src), part(dst), loc).wait()

    def xcopy(n, u, way, b=None):
        src, dst = (0, 3) if way == 0 else (1, 2)

        def part(r):
            return rows.at[n, r, u] if b is None else rows.at[n, r, 0, :, pl.ds(b * HEAD, HEAD)]
        s, r = (xs3.at[n, way], xr3.at[n, way]) if b == 0 else (xs.at[n, u, way], xr.at[n, u, way])
        return remote(part(src), part(dst), s, r, xdev(1 if way == 0 else -1))

    def picked(m, size, shift):
        row = lax.broadcasted_iota(jnp.int32, (size, NE), 0)
        e_of = z * NP + lax.rem(p + lax.shift_right_logical(row, shift), NP)
        pick = jnp.where(lax.broadcasted_iota(jnp.int32, (size, NE), 1) == e_of, 1.0, 0.0).astype(BF16)
        within = lax.broadcasted_iota(jnp.int32, (size, T), 0) & ((1 << shift) - 1)
        return dot(pick, m[0:NE]), dot(pick, m[NE:2 * NE]), within.astype(F32)

    def build(pos):
        pair, b = divmod(pos, 2)
        m = meta[pos]
        s, gx, within = picked(m, ROWS, 5)
        tail = jnp.logical_and(s + float(TAIL * pos - HEAD) == within, s >= float(HEAD))
        pt[:, pl.ds(pos * T, T)] = jnp.where(tail, 1.0, 0.0).astype(BF16)
        wtt[pl.ds(pos * T, T), :] = jnp.where(tail, gx, 0.0).T.astype(BF16)
        head = jnp.logical_and(s + float(HEAD * b) == within, s < float(HEAD))
        wt[pair, pl.ds(b * T, T), :] = jnp.where(head, gx, 0.0).T.astype(BF16)
        if pair > 0:
            pm[pair - 1, :, pl.ds(b * T, T)] = jnp.where(head, 1.0, 0.0).astype(BF16)
        else:
            s, gx, within = picked(m, NP * HEAD, 4)
            ph[b] = jnp.where(s == within, 1.0, 0.0).astype(BF16)

    def gather_half(n, b):
        for ab in range(2):
            y = dot(ph[b], zbuf[n, ab, b]).astype(BF16)
            yout[n, ab, 0, :, b * HEAD:(b + 1) * HEAD] = y.reshape(NP, HEAD, w)

    def gather(n, u):
        @pl.when(jnp.logical_and(u > 0, u < U - 1))
        def _():
            for ab in range(2):
                y = dot(pm[u - 1], zbuf[n, ab, pl.ds(2 * u, 2)].reshape(2 * T, w)).astype(BF16)
                yout[n, ab, u] = y.reshape(NP, B, w)

        @pl.when(u == U - 1)
        def _():
            for ab in range(2):
                yout[n, ab, u] = dot(pt[...], zbuf[n, ab].reshape(NZ * T, w)).astype(BF16).reshape(NP, B, w)

    def up_to(n, u, first):
        def one(r, _):
            acc[u] = acc[u] + dot(rows[n, r, u].reshape(ROWS, w), wgu[pl.ds(cols(r, n), w), :])
            return 0
        lax.fori_loop(first, first + 2, one, 0)

    def activate(u):
        def one(i, _):
            at = pl.ds(pl.multiple_of(i * 64, 64), 64)
            gate = acc[u, at, 0:FF]
            hid[u, at, :] = (gate / (1.0 + jnp.exp(-gate)) * acc[u, at, FF:2 * FF]).astype(BF16)
            return 0
        lax.fori_loop(0, ROWS // 64, one, 0)

    def on(i):
        return pl.when(jnp.logical_and(i >= 0, i < U * C))

    def x2copy(n, u, way):
        return remote(yout.at[n, way, u], pxin.at[n, 1 - way, u], xs2.at[n, u, way], xr2.at[n, u, way],
                      xdev(1 if way == 0 else -1))

    def down(n, u, r):
        return dot(hid[u], wd[:, pl.ds(cols(r, n), w)])

    def z2copy(n, way, h):
        slot = (3 + h) if way == 0 else (5 - h)
        part = pl.ds(0, 2) if h > 1 else pl.ds(way, 1)
        return remote(zbuf.at[n, part, POS[slot]], zrec.at[n, way, h - 1, part],
                      zs2.at[n, way, h - 1], zr2.at[n, way, h - 1], zdev(1 if way == 0 else -1))

    def z2start(n, h):
        for way in range(2):
            z2copy(n, way, h).start()

    def z2add(n, h):
        for way in range(2):
            z2copy(n, way, h).wait_recv()
            slot = POS[(4 + h) if way == 0 else (4 - h)]
            for ab in range(2) if h > 1 else (way,):
                zbuf[n, ab, slot] = (zbuf[n, ab, slot].astype(F32) + zrec[n, way, h - 1, ab].astype(F32)).astype(BF16)

    def combine(n, u):
        @pl.when(u < U - 1)
        def _():
            at = pl.ds(2 * u, 2)
            for ab in range(2):
                c = dot(wt[u], yret[n, ab, u].reshape(ROWS, w)).reshape(2, T, w)
                before = jnp.where(u == 0, 0.0, zbuf[n, ab, at].astype(F32))
                zbuf[n, ab, at] = (before + c).astype(BF16)

        @pl.when(u == U - 1)
        def _():
            for ab in range(2):
                c = dot(wtt[...], yret[n, ab, u].reshape(ROWS, w)).reshape(NZ, T, w)
                zbuf[n, ab, 0:2] = (zbuf[n, ab, 0:2].astype(F32) + c[0:2]).astype(BF16)
                zbuf[n, ab, 2:8] = c[2:8].astype(BF16)

    def fcopy(n):
        return remote(fin_s.at[n], fin_r.at[n], fs.at[n], fr.at[n], xdev(1))

    for n in range(C):
        zstart(n, 1)
    build(0)

    def first(n, _):
        gather_half(n, 0)
        ystart(yout, rows, ys4.at[n], yr4.at[n], yl4.at[n], n, 0, 1, 0)
        return 0

    lax.fori_loop(0, C, first, 0)

    def step(i, _):
        def out_at(i):
            late = i - (U - 2) * C
            u = jnp.where(late < 0, lax.div(i, C) + 1, jnp.where(late < C // 2, 0, U - 1))
            return u, jnp.where(late < 0, lax.rem(i, C), jnp.where(late < C // 2, 2 * late, late - C // 2))

        def on_out(i):
            return pl.when(jnp.logical_and(i >= 0, i < S))
        j, k = i - LY, i - LX
        u, n = out_at(i)
        ju, jn = out_at(j)
        ku, kn = out_at(k)

        @pl.when(i < C)
        def _():
            ywait(yout, rows, ys4.at[i], yr4.at[i], yl4.at[i], i, 0, 0)
            for way in range(2):
                xcopy(i, 0, way, 0).start()

        @on_out(i)
        def _():
            for h in range(1, 4):
                @pl.when(u == h)
                def _():
                    zwait(n, h)
                    zstart(n, h + 1)

                    @pl.when(n == 0)
                    def _():
                        build(POS[h])
                        build(POS[NZ - h])

            @pl.when(u == 0)
            def _():
                for m in range(2):
                    zwait(n + m, 4)
                    if m == 0:
                        @pl.when(n == 0)
                        def _():
                            build(POS[4])
                    gather_half(n + m, 1)
                    ystart(yout, rows, ys.at[n + m, 0], yr.at[n + m, 0], yl.at[n + m, 0], n + m, 0, 1, 1)

            @pl.when(u > 0)
            def _():
                gather(n, u)
                ystart(yout, rows, ys.at[n, u], yr.at[n, u], yl.at[n, u], n, u, 1)

        @pl.when(i == LY)
        def _():
            w_copies[0].wait()
            w_copies[1].wait()

        @on_out(j)
        def _():
            @pl.when(ju == 0)
            def _():
                for m in range(2):
                    ywait(yout, rows, ys.at[jn + m, 0], yr.at[jn + m, 0], yl.at[jn + m, 0], jn + m, 0, 1)
                    for way in range(2):
                        xcopy(jn + m, 0, way, 1).start()
                    up_to(jn + m, 0, 0)

            @pl.when(ju > 0)
            def _():
                ywait(yout, rows, ys.at[jn, ju], yr.at[jn, ju], yl.at[jn, ju], jn, ju)
                for way in range(2):
                    xcopy(jn, ju, way).start()
                up_to(jn, ju, 0)

        @on_out(k)
        def _():
            @pl.when(ku == 0)
            def _():
                for m in range(2):
                    for b in range(2):
                        for way in range(2):
                            xcopy(kn + m, 0, way, b).wait_recv()
                    up_to(kn + m, 0, 2)

                @pl.when(kn == C - 2)
                def _():
                    activate(0)

            @pl.when(ku > 0)
            def _():
                for way in range(2):
                    xcopy(kn, ku, way).wait_recv()
                up_to(kn, ku, 2)

                @pl.when(kn == C - 1)
                def _():
                    activate(ku)

        r = i - R0
        rj, rk = r - KX, r - KY

        def unit(q):
            return jnp.where(q == 0, 0, U - q)
        ru, rn = unit(lax.div(r, C)), lax.rem(r, C)
        rju, rjn = unit(lax.div(rj, C)), lax.rem(rj, C)
        rku, rkn = unit(lax.div(rk, C)), lax.rem(rk, C)

        @pl.when(r == 0)
        def _():
            w_copies[2].wait()

        @on(r)
        def _():
            @pl.when(ru == 0)
            def _():
                yall(yout, rows, ys4.at[rn], yr4.at[rn], rn, 0, 0).wait_send()
                yall(yout, rows, ys.at[rn, 0], yr.at[rn, 0], rn, 0, 1).wait_send()

            @pl.when(ru > 0)
            def _():
                yall(yout, rows, ys.at[rn, ru], yr.at[rn, ru], rn, ru).wait_send()
            for way in range(2):
                yout[rn, way, ru] = down(rn, ru, 2 + way).astype(BF16).reshape(NP, B, w)
                x2copy(rn, ru, way).start()

        @on(rj)
        def _():
            @pl.when(rju == 0)
            def _():
                for ab in range(2):
                    for b in range(2):
                        xcopy(rjn, 0, ab, b).wait_send()

            @pl.when(rju > 0)
            def _():
                for ab in range(2):
                    xcopy(rjn, rju, ab).wait_send()
            for ab in range(2):
                x2copy(rjn, rju, 1 - ab).wait_recv()
                both = down(rjn, rju, ab) + pxin[rjn, ab, rju].reshape(ROWS, w).astype(F32)
                rows[rjn, ab, rju] = both.astype(BF16).reshape(NP, B, w)
            ystart(rows, yret, ys2.at[rjn, rju], yr2.at[rjn, rju], yl2.at[rjn, rju], rjn, rju, -1)

        @on(rk)
        def _():
            ywait(rows, yret, ys2.at[rkn, rku], yr2.at[rkn, rku], yl2.at[rkn, rku], rkn, rku)

            @pl.when(rku == 0)
            def _():
                for way in range(2):
                    for h in range(1, 5):
                        zcopy(rkn, way, h).wait_send()
            combine(rkn, rku)
            for v, h in ((4, 1), (3, 2), (2, 3), (1, 4)):
                @pl.when(rku == v)
                def _():
                    if h > 1:
                        z2add(rkn, h - 1)
                    z2start(rkn, h)
        return 0

    lax.fori_loop(0, R0 + U * C + KY, step, 0)
    for h in range(1, 5):
        for way in range(2 if h < 4 else 1):
            mcopy(way, h).wait_send()

    def finish(n, _):
        tot = []
        for way in range(2):
            z2copy(n, way, 4).wait_recv()
        for ab in range(2):
            tot.append(zbuf[n, ab, 0].astype(F32) + zrec[n, 0, 3, ab].astype(F32) + zrec[n, 1, 3, ab].astype(F32))
        fin_s[n] = tot[1].astype(BF16)
        fcopy(n).start()
        fin_a[n] = tot[0]
        return 0

    lax.fori_loop(0, C, finish, 0)

    def write(n, _):
        fcopy(n).wait_recv()
        out[:, pl.ds(pl.multiple_of(n * w, w), w)] = (fin_a[n] + fin_r[n].astype(F32)).astype(BF16)
        return 0

    lax.fori_loop(0, C, write, 0)

    def left_back(n, _):
        for way in range(2):
            for h in range(1, 5):
                z2copy(n, way, h).wait_send()

        def unit(u, _):
            yall(rows, yret, ys2.at[n, u], yr2.at[n, u], n, u).wait_send()
            for way in range(2):
                x2copy(n, u, way).wait_send()
            return 0
        lax.fori_loop(0, U, unit, 0)
        fcopy(n).wait_send()
        return 0

    lax.fori_loop(0, C, left_back, 0)


def local(tokens, routing, gate_weights, w_gate, w_up, w_down):
    T, D = tokens.shape
    FF = w_gate.shape[2]
    w = D // NX // C
    dma = pltpu.SemaphoreType.DMA
    vm = pl.BlockSpec(memory_space=pltpu.VMEM)
    anyw = pl.BlockSpec(memory_space=pl.ANY)
    return pl.pallas_call(
        kernel,
        out_shape=jax.ShapeDtypeStruct((T, D // NX), BF16),
        in_specs=[vm, vm, vm, anyw, anyw, anyw],
        out_specs=vm,
        scratch_shapes=[
            pltpu.VMEM((C, 2, NZ, T, w), BF16),
            pltpu.VMEM((NZ, 128, T), BF16),
            pltpu.VMEM((U - 2, ROWS, 2 * T), BF16),
            pltpu.VMEM((ROWS, NZ * T), BF16),
            pltpu.VMEM((2, NP * HEAD, T), BF16),
            pltpu.VMEM((U - 1, 2 * T, ROWS), BF16),
            pltpu.VMEM((NZ * T, ROWS), BF16),
            pltpu.VMEM((C, 2, U, NP, B, w), BF16),
            pltpu.VMEM((C, 4, U, NP, B, w), BF16),
            pltpu.VMEM((U, ROWS, 2 * FF), F32),
            pltpu.VMEM((D, 2 * FF), BF16),
            pltpu.VMEM((FF, D), BF16),
            pltpu.VMEM((U, ROWS, FF), BF16),
            pltpu.VMEM((C, 2, U, NP, B, w), BF16),
            pltpu.VMEM((C, 2, U, NP, B, w), BF16),
            pltpu.VMEM((C, 2, 4, 2, T, w), BF16),
            pltpu.VMEM((C, T, w), F32),
            pltpu.VMEM((C, T, w), BF16),
            pltpu.VMEM((C, T, w), BF16),
            dma((3,)),
            dma((C, 2, 4)), dma((C, 2, 4)),
            dma((2, 4)), dma((2, 4)),
            dma((C, U)), dma((C, U)), dma((C, U)),
            dma((C, U, 2)), dma((C, U, 2)),
            dma((C, 2, 4)), dma((C, 2, 4)),
            dma((C, U)), dma((C, U)), dma((C, U)),
            dma((C,)), dma((C,)), dma((C,)),
            dma((C, 2)), dma((C, 2)),
            dma((C, U, 2)), dma((C, U, 2)),
            dma((C,)), dma((C,)),
        ],
        compiler_params=pltpu.CompilerParams(
            collective_id=0, has_side_effects=True, vmem_limit_bytes=60 * 1024 * 1024
        ),
        cost_estimate=pl.CostEstimate(flops=16_000_000_000, bytes_accessed=11_000_000, transcendentals=500_000),
    )(routing.T, gate_weights.T, tokens, w_gate, w_up, w_down)


def solution(mesh):
    return jax.shard_map(
        local,
        mesh=mesh,
        in_specs=(
            P("expert", None),
            P("expert", None),
            P("expert", None),
            P("expert", None, "tensor"),
            P("expert", None, "tensor"),
            P("expert", "tensor", None),
        ),
        out_specs=P("expert", "tensor"),
        check_vma=False,
    )
```
